32 devices in a mesh: groups: 2 (over y), expert: 8 (over z, x), dp: 2 (over core).
Axes of the slice: x: 2, y: 2, z: 4, core: 2. Of those that a mesh axis runs over, the one named last changes fastest.
Arguments:
- hidden_states: bfloat16 [512, 3584], P(('groups', 'expert', 'dp')), parts along dimension 0, may hold values from -6 to 6
- out_grad: bfloat16 [512, 3584], P(('groups', 'expert', 'dp')), parts along dimension 0, may hold values from -6 to 6
- expert_ids: int32 [512, 1], P(('groups', 'expert', 'dp')), parts along dimension 0, may hold values from 0 to 15; in each aligned block of 16 rows (0 to 15, 16 to 31, ...) at most 2 rows name the same one
- gate_probs: bfloat16 [512, 1], P(('groups', 'expert', 'dp')), parts along dimension 0, may hold values from 0.5 to 2.5
- block_expert: int32 [128], replicated, may hold values from 0 to 15, as said below
- gate_weight: bfloat16 [128, 3584, 128], P('expert', 'dp'), may hold values from -0.09375 to 0.09375
- up_weight: bfloat16 [128, 3584, 128], P('expert', 'dp'), may hold values from -0.09375 to 0.09375
- down_weight: bfloat16 [128, 128, 3584], P('expert', None, 'dp'), may hold values from -0.1875 to 0.1875
Outputs:
- input_grad: bfloat16 [512, 3584], P(('groups', 'expert', 'dp')), parts along dimension 0
- gate_grad: bfloat16 [256, 3584, 128], P(('groups', 'expert'), 'dp'), parts along dimension 0
- up_grad: bfloat16 [256, 3584, 128], P(('groups', 'expert'), 'dp'), parts along dimension 0
- down_grad: bfloat16 [256, 128, 3584], P(('groups', 'expert'), None, 'dp'), parts along dimension 0
The draws below stay inside these ranges and needn't reach their ends.
There are 2 independent parts, one for each index of `groups`. The reference program is written for one: setup_inputs(seed, part) draws one part's arguments, and reference() takes and returns one part's arrays. A program takes and returns all parts, laid end to end along the dimension named above; an argument that names none is the same for every part. Nothing has to cross between parts.
Inputs may be any that keep to these rules, and one draw needn't show every extreme that they name: `expert_ids`: each row names 1 different experts. In the rows of one device no expert is named by more than 2 rows, and in some device's rows an expert is named by exactly 2. `block_expert`: each expert is named by exactly 8 entries.
All inputs are finite; a program needn't handle non-finite values.
Results may differ from the reference program's by a relative error of at most 0.0067.
Values may be sent and summed in bfloat16 or wider, within the bound.
A program may use at most 256 MiB of HBM per device.

```python
import math
import jax
import jax.numpy as jnp
import numpy as np
from jax import lax

D = 3584
FF = 1024
BLOCK = 128
EXPERTS = 16
TOPK = 1
TOK_DEV = 16
SLOT = 2
NB = 128
TOKENS = 256
N_EXPERT = 8
N_DP = 2


def draw_block_expert(key, part):
    key = jax.random.fold_in(key, 7)
    shuffled = jax.random.permutation(key, EXPERTS * FF // BLOCK)
    return (shuffled // (FF // BLOCK)).astype(jnp.int32)


def block_scale(stream_key, extent, shards, low, high):
    loudness = 1.0
    for position, shards_of in shards:
        draws = jax.random.uniform(jax.random.fold_in(jax.random.fold_in(stream_key, 6), position), (shards_of,), jnp.float32, low / len(shards), high / len(shards))
        loudness = loudness * jnp.repeat(jnp.exp(draws), extent[position] // shards_of).reshape((-1,) + (1,) * (len(extent) - 1 - position))
    return loudness


def routed_block(rng, own, number, rows, amount, top, reach, skew):
    sequence = jax.random.permutation(rng, amount)
    packed, common = load_shares(amount, rows * top, reach, skew, True), load_shares(amount, rows * top, reach, skew, False)
    places = jnp.arange(amount)

    def named(lengths, offset_by):
        used = int((lengths > 0).sum())
        fixed = max(1, used // 4)
        shifted = fixed + (places - fixed + offset_by * (used - fixed)) % max(1, amount - fixed)
        return jnp.zeros((amount,), jnp.int32).at[sequence[jnp.where(places < fixed, places, shifted)]].set(jnp.asarray(lengths, jnp.int32))

    lengths = jnp.where(number % 4 == 0, named(packed, number // 4), named(common, number - number // 4 - 1))
    mixed = jax.random.permutation(jax.random.fold_in(own, 3), amount)
    giver, receiver = mixed[0:amount // 2 * 2:2], mixed[1:amount // 2 * 2:2]
    slack = jnp.minimum(lengths[giver] - 1, reach - lengths[receiver]) // 2
    slack = jnp.where((giver == sequence[0]) | (receiver == sequence[0]) | (lengths[receiver] == 0), 0, jnp.maximum(slack, 0))
    shifted = jax.random.randint(jax.random.fold_in(own, 4), (amount // 2,), 0, 1 << 20) % (slack + 1)
    lengths = lengths.at[giver].add(-shifted).at[receiver].add(shifted)
    items = jnp.searchsorted(jnp.cumsum(lengths), jnp.arange(rows * top), side="right").astype(jnp.int32)
    grid = items.reshape(top, rows).T
    grid = grid[jax.random.permutation(jax.random.fold_in(own, 1), rows)]
    offset_by = jax.random.randint(jax.random.fold_in(own, 2), (rows, 1), 0, top)
    return jnp.take_along_axis(grid, (jnp.arange(top)[None, :] + offset_by) % top, axis=1)


def load_shares(amount, total, limit, lean, full):
    loads = [(1 << 20) // math.isqrt(standing ** lean) + 1 for standing in range(1, amount + 1)]
    largest = limit if full else min(limit, max(-(-total // amount), total * loads[0] // sum(loads)))
    least = 1 if total - largest >= amount - 1 else 0
    given, surplus = [largest] + [least] * (amount - 1), total - largest - least * (amount - 1)
    while surplus > 0:
        movable = [i for i in range(1, amount) if given[i] < largest] or [i for i in range(1, amount) if given[i] < limit]
        pool, budget = sum([loads[i] for i in movable]), surplus
        for i in movable:
            addition = min(limit - given[i], max(1, budget * loads[i] // pool), surplus)
            given[i] = given[i] + addition
            surplus = surplus - addition
    return np.array(given)


def bell_draw(stream_key, extent, deviation, reach, cuts=(), kind=jnp.bfloat16):
    factor_of = block_scale(stream_key, extent, cuts, -0.22, 0.18) if cuts else 1.0
    result = jax.random.normal(stream_key, extent, jnp.float32) * deviation * factor_of
    return jnp.minimum(jnp.maximum(result, -reach), reach).astype(kind)


def setup_inputs(seed: int = 0, part: int = 0) -> dict:
    key_list = jax.random.split(jax.random.key(seed), 9)
    part_keys = jax.random.split(jax.random.fold_in(key_list[8], part), 9)
    hidden_states = bell_draw(part_keys[0], (TOKENS, D), 1.0, 6.0, ((0, 16),))
    out_grad = bell_draw(part_keys[1], (TOKENS, D), 1.0, 6.0, ((0, 16),))
    expert_ids_keys = jax.random.split(jax.random.fold_in(part_keys[2], 1), TOKENS // TOK_DEV)
    expert_ids_turns = jax.random.permutation(jax.random.fold_in(part_keys[2], 3), TOKENS // TOK_DEV)
    expert_ids = jax.vmap(lambda own, number: routed_block(jax.random.fold_in(part_keys[2], 2), own, number, TOK_DEV, EXPERTS, TOPK, SLOT, 2))(expert_ids_keys, expert_ids_turns).reshape((TOKENS, TOPK))
    gate_probs = jnp.clip(0.5 + 2.0 * jax.random.uniform(part_keys[3], (TOKENS, TOPK), jnp.float32) ** block_scale(part_keys[3], (TOKENS, TOPK), ((0, 16),), -0.2, 0.2), 0.5, 2.5).astype(jnp.bfloat16)
    block_expert = draw_block_expert(jax.random.fold_in(key_list[8], 71), part)
    gate_weight = bell_draw(key_list[5], (NB, D, BLOCK), D ** -0.5, 0.09375, ((0, 8), (1, 2)))
    up_weight = bell_draw(key_list[6], (NB, D, BLOCK), D ** -0.5, 0.09375, ((0, 8), (1, 2)))
    down_weight = bell_draw(key_list[7], (NB, BLOCK, D), FF ** -0.5, 0.1875, ((0, 8), (2, 2)))
    return dict(hidden_states=hidden_states, out_grad=out_grad, expert_ids=expert_ids, gate_probs=gate_probs, block_expert=block_expert, gate_weight=gate_weight, up_weight=up_weight, down_weight=down_weight)


def rounded(value):
    return lax.optimization_barrier(value.astype(jnp.bfloat16)).astype(jnp.float32)


def reference(hidden_states, out_grad, expert_ids, gate_probs, block_expert, gate_weight, up_weight, down_weight):
    tokens = hidden_states.shape[0]
    per_expert = FF // BLOCK
    capacity = min(tokens, N_EXPERT * N_DP * SLOT)
    inputs = hidden_states.astype(jnp.float32)
    cotangent = out_grad.astype(jnp.float32)
    half_of = (jnp.arange(tokens, dtype=jnp.int32) // TOK_DEV) % N_DP
    input_grad = jnp.zeros(inputs.shape, jnp.float32)
    gate_grad = jnp.zeros(gate_weight.shape, jnp.float32)
    up_grad = jnp.zeros(up_weight.shape, jnp.float32)
    down_grad = jnp.zeros(down_weight.shape, jnp.float32)
    for expert in range(EXPERTS):
        hits = expert_ids == expert
        present = jnp.any(hits, axis=1)
        share = jnp.sum(jnp.where(hits, gate_probs.astype(jnp.float32), jnp.float32(0.0)), axis=1)
        row_index = jnp.argsort(jnp.where(present, 0, 1).astype(jnp.int32), stable=True)[:capacity].astype(jnp.int32)
        keep = present[row_index][:, None]
        x_rows = jnp.where(keep, inputs[row_index], jnp.float32(0.0))
        scaled = rounded(share[row_index][:, None] * cotangent[row_index])
        block_index = jnp.argsort(jnp.where(block_expert == expert, 0, 1).astype(jnp.int32), stable=True)[:per_expert].astype(jnp.int32)
        w_gate = gate_weight[block_index].astype(jnp.float32)
        w_up = up_weight[block_index].astype(jnp.float32)
        w_down = down_weight[block_index].astype(jnp.float32)
        gate_pre = jnp.einsum("rd,pdf->rpf", x_rows, w_gate)
        up_pre = jnp.einsum("rd,pdf->rpf", x_rows, w_up)
        sigmoid_gate = jax.nn.sigmoid(gate_pre)
        swish_gate = gate_pre * sigmoid_gate
        hidden = rounded(swish_gate * up_pre)
        hidden_grad = jnp.einsum("rd,pfd->rpf", scaled, w_down)
        d_gate = rounded(hidden_grad * up_pre * sigmoid_gate * (1.0 + gate_pre * (1.0 - sigmoid_gate)))
        d_up = rounded(hidden_grad * swish_gate)
        block_part = rounded(jnp.einsum("rpf,pdf->rpd", d_gate, w_gate) + jnp.einsum("rpf,pdf->rpd", d_up, w_up))
        input_grad = input_grad.at[row_index].add(jnp.sum(block_part, axis=1))
        sum_gate = jnp.zeros(w_gate.shape, jnp.float32)
        sum_up = jnp.zeros(w_up.shape, jnp.float32)
        sum_down = jnp.zeros(w_down.shape, jnp.float32)
        for dp_half in range(N_DP):
            half_mask = (half_of[row_index] == dp_half).astype(jnp.float32)[:, None]
            masked_rows = x_rows * half_mask
            sum_gate = sum_gate + rounded(jnp.einsum("rd,rpf->pdf", masked_rows, d_gate))
            sum_up = sum_up + rounded(jnp.einsum("rd,rpf->pdf", masked_rows, d_up))
            sum_down = sum_down + rounded(jnp.einsum("rpf,rd->pfd", hidden, scaled * half_mask))
        gate_grad = gate_grad.at[block_index].set(sum_gate)
        up_grad = up_grad.at[block_index].set(sum_up)
        down_grad = down_grad.at[block_index].set(sum_down)
    return (input_grad.astype(jnp.bfloat16), gate_grad.astype(jnp.bfloat16), up_grad.astype(jnp.bfloat16), down_grad.astype(jnp.bfloat16))
```

```python
import functools

import jax
import jax.numpy as jnp
from jax import lax
from jax.experimental import pallas as pl
from jax.experimental.pallas import tpu as pltpu
from jax.sharding import PartitionSpec as P

SLOT = 2
F32 = jnp.float32
BF16 = jnp.bfloat16
LANES = 128
ROWS_DIM = (((0,), (0,)), ((), ()))
LAST_DIM = (((1,), (1,)), ((), ()))


def activations(gate_pre, up_pre, hidden_grad):
    s = jax.nn.sigmoid(gate_pre)
    swish = gate_pre * s
    hidden = (swish * up_pre).astype(BF16)
    d_gate = (hidden_grad * up_pre * s * (1.0 + gate_pre * (1.0 - s))).astype(BF16)
    d_up = (hidden_grad * swish).astype(BF16)
    return hidden, d_gate, d_up


def tile_of(width):
    for tile in (256, 128):
        if width % tile == 0:
            return tile
    return width


def route_kernel(
    n_e, slots,
    experts, x_ref, g_ref, ids_ref, gates_ref, wg_hbm, wu_hbm, wd_hbm,
    out_ref, sel_hbm, dgu_ref, hid_ref,
    wg, wu, wd, pack, buf, pick, sel, pre, pre_in, part_rows, total, sent,
    x_in, up_in, down_in, up_out, down_out, acc, fin_out, fin_in,
    w_sem, sel_sem, pair_sem, recv_sem, x_sem, up_sem, down_sem, pre_sem, pre_recv,
    xs_sem, xs_recv, us_sem, us_recv, ds_sem, ds_recv, fin_sem,
):
    blocks, half, ff = wg.shape
    tok = x_ref.shape[0]
    pair = 2 * tok
    tokens = n_e * pair
    n_z = n_e // 2
    me, d = lax.axis_index("expert"), lax.axis_index("dp")
    z, col = me // 2, me % 2
    has_up, has_down = z < n_z - 1, z > 0
    core = {"dp": 1 - d}
    side = {"expert": me + 1 - 2 * col}
    above = {"expert": jnp.minimum(me + 2, n_e - 2 + col)}
    below = {"expert": jnp.maximum(me - 2, col)}

    def weight_copies(j):
        return [
            pltpu.make_async_copy(src.at[j], dst.at[j], w_sem.at[k, j])
            for k, (src, dst) in enumerate(((wg_hbm, wg), (wu_hbm, wu), (wd_hbm, wd)))
        ]

    def remote(src, dst, send, recv, where):
        return pltpu.make_async_remote_copy(
            src_ref=src, dst_ref=dst, send_sem=send, recv_sem=recv,
            device_id=where, device_id_type=pl.DeviceIdType.MESH,
        )

    barrier = pltpu.get_barrier_semaphore()
    for where in (core, side):
        pl.semaphore_signal(barrier, inc=1, device_id=where, device_id_type=pl.DeviceIdType.MESH)

    @pl.when(has_up)
    def _():
        pl.semaphore_signal(barrier, inc=1, device_id=above, device_id_type=pl.DeviceIdType.MESH)

    @pl.when(has_down)
    def _():
        pl.semaphore_signal(barrier, inc=1, device_id=below, device_id_type=pl.DeviceIdType.MESH)

    scaled = (gates_ref[...].astype(F32) * g_ref[...].astype(F32)).astype(BF16)
    named = jnp.broadcast_to(ids_ref[...].astype(F32), (tok, LANES)).astype(BF16)
    for h in range(2):
        pack[h, :, 0:half] = x_ref[:, h * half:(h + 1) * half]
        pack[h, :, half:2 * half] = scaled[:, h * half:(h + 1) * half]
        pack[h, :, 2 * half:] = named

    pl.semaphore_wait(barrier, 2 + has_up.astype(jnp.int32) + has_down.astype(jnp.int32))

    mine = pl.ds(pl.multiple_of(me * pair + d * tok, 16), tok)
    swap = remote(pack.at[1 - d], buf.at[mine], pair_sem.at[0], pair_sem.at[1], core)
    swap.start()
    buf[mine, :] = pack[d]

    @pl.loop(0, blocks)
    def _(j):
        for copy in weight_copies(j):
            copy.start()

    swap.wait()

    def rows(b):
        return pl.ds(pl.multiple_of(b * pair, 16), pair)

    def hop(b, send, where):
        at = buf.at[rows(b)]
        return remote(at, at, send, recv_sem.at[b], where)

    hop(me, x_sem.at[z], side).start()

    @pl.when(has_up)
    def _():
        hop(me, up_sem.at[z], above).start()

    @pl.when(has_down)
    def _():
        hop(me, down_sem.at[z], below).start()

    for h in range(1, n_z):
        @pl.when(z - h >= 0)
        def _():
            b = me - 2 * h
            hop(b, x_sem.at[z - h], side).wait_recv()

            @pl.when(has_up)
            def _():
                hop(b, up_sem.at[z - h], above).start()

            hop(b, x_sem.at[z - h], side).start()

        @pl.when(z + h < n_z)
        def _():
            b = me + 2 * h
            hop(b, x_sem.at[z + h], side).wait_recv()

            @pl.when(has_down)
            def _():
                hop(b, down_sem.at[z + h], below).start()

            hop(b, x_sem.at[z + h], side).start()

    for k in range(n_z):
        hop(2 * k + 1 - col, x_sem.at[k], side).wait_recv()

    id_cols = buf[:, 2 * half:].astype(F32)
    id_row = id_cols.T[0:1, :]
    earlier = lax.broadcasted_iota(jnp.int32, (tokens, tokens), 0) < lax.broadcasted_iota(
        jnp.int32, (tokens, tokens), 1
    )
    same = (id_cols[:, 0:1] == id_row) & earlier
    rank = jnp.sum(same.astype(F32), axis=0, keepdims=True)
    key = id_row * float(slots) + rank
    place = lax.broadcasted_iota(jnp.int32, (slots, tokens), 0).astype(F32)
    for j in range(blocks):
        base = experts[me * blocks + j].astype(F32) * float(slots)
        pick[j * slots:(j + 1) * slots, :] = (key == place + base).astype(F32).astype(BF16)

    step = tile_of(2 * half)

    @pl.loop(0, 2 * half // step)
    def _(c):
        cols = pl.ds(pl.multiple_of(c * step, step), step)
        sel[:, cols] = jnp.dot(pick[...], buf[:, cols], preferred_element_type=F32).astype(BF16)

    sel_copy = pltpu.make_async_copy(sel, sel_hbm, sel_sem)
    sel_copy.start()

    def swap_pre(j):
        return remote(pre.at[j], pre_in.at[j], pre_sem.at[j], pre_recv.at[j], core)

    @pl.loop(0, blocks)
    def _(j):
        for copy in weight_copies(j):
            copy.wait()
        at = pl.ds(pl.multiple_of(j * slots, 16), slots)
        xs, gs = sel[at, 0:half], sel[at, half:2 * half]
        pre[j, :, 0:ff] = jnp.dot(xs, wg[j], preferred_element_type=F32)
        pre[j, :, ff:2 * ff] = jnp.dot(xs, wu[j], preferred_element_type=F32)
        pre[j, :, 2 * ff:] = lax.dot_general(gs, wd[j], LAST_DIM, preferred_element_type=F32)
        swap_pre(j).start()

    @pl.loop(0, blocks)
    def _(j):
        swap_pre(j).wait()
        at = pl.ds(pl.multiple_of(j * slots, 16), slots)
        both = pre[j] + pre_in[j]
        hidden, d_gate, d_up = activations(both[:, 0:ff], both[:, ff:2 * ff], both[:, 2 * ff:])
        hid_ref[at, :] = hidden
        dgu_ref[at, 0:ff] = d_gate
        dgu_ref[at, ff:] = d_up
        part = lax.dot_general(d_gate, wg[j], LAST_DIM, preferred_element_type=F32)
        part = part + lax.dot_general(d_up, wu[j], LAST_DIM, preferred_element_type=F32)
        part_rows[at, :] = part.astype(BF16)

    step_out = tile_of(half)

    @pl.loop(0, half // step_out)
    def _(c):
        cols = pl.ds(pl.multiple_of(c * step_out, step_out), step_out)
        tile = lax.dot_general(pick[...], part_rows[:, cols], ROWS_DIM, preferred_element_type=F32)
        total[:, cols] = tile
        sent[:, cols] = tile.astype(BF16)

    def side_send(k):
        return remote(sent.at[rows(2 * k + 1 - col)], x_in.at[k], xs_sem.at[k], xs_recv.at[k], side)

    def up_send(k):
        return remote(up_out.at[k], up_in.at[k], us_sem.at[k], us_recv.at[k], above)

    def down_send(k):
        return remote(down_out.at[k], down_in.at[k], ds_sem.at[k], ds_recv.at[k], below)

    for h in range(n_z - 1, 0, -1):
        @pl.when(z + h < n_z)
        def _():
            side_send(z + h).start()

        @pl.when(z - h >= 0)
        def _():
            side_send(z - h).start()

    side_send(z).start()

    def own_sum(k):
        side_send(k).wait_recv()
        acc[...] = total[rows(2 * k + col), :] + x_in[k].astype(F32)

    for h in range(n_z - 1, 0, -1):
        @pl.when(z + h < n_z)
        def _():
            k = z + h
            own_sum(k)

            @pl.when(has_down)
            def _():
                up_send(k).wait_recv()
                acc[...] += up_in[k].astype(F32)

            up_out[k] = acc[...].astype(BF16)
            up_send(k).start()

        @pl.when(z - h >= 0)
        def _():
            k = z - h
            own_sum(k)

            @pl.when(has_up)
            def _():
                down_send(k).wait_recv()
                acc[...] += down_in[k].astype(F32)

            down_out[k] = acc[...].astype(BF16)
            down_send(k).start()

    own_sum(z)

    @pl.when(has_down)
    def _():
        up_send(z).wait_recv()
        acc[...] += up_in[z].astype(F32)

    @pl.when(has_up)
    def _():
        down_send(z).wait_recv()
        acc[...] += down_in[z].astype(F32)

    fin_out[...] = acc[...].astype(BF16).reshape(2, tok, half)
    last = remote(fin_out.at[1 - d], fin_in, fin_sem.at[0], fin_sem.at[1], core)
    last.start()
    out_ref[:, pl.ds(pl.multiple_of(d * half, LANES), half)] = fin_out[d]
    last.wait()
    out_ref[:, pl.ds(pl.multiple_of((1 - d) * half, LANES), half)] = fin_in[...]

    for k in range(n_z):
        hop(2 * k + col, x_sem.at[k], side).wait_send()
        side_send(k).wait_send()

        @pl.when(has_up & (z >= k))
        def _():
            hop(2 * k + col, up_sem.at[k], above).wait_send()

        @pl.when(has_down & (z <= k))
        def _():
            hop(2 * k + col, down_sem.at[k], below).wait_send()

        @pl.when(z < k)
        def _():
            up_send(k).wait_send()

        @pl.when(z > k)
        def _():
            down_send(k).wait_send()

    sel_copy.wait()


def grads_kernel(sel, dgu, hid, gate_out, up_out, down_out):
    half, ff = gate_out.shape[1:]
    both = lax.dot_general(sel[:, 0:half], dgu[...], ROWS_DIM, preferred_element_type=F32)
    gate_out[0] = both[:, 0:ff].astype(BF16)
    up_out[0] = both[:, ff:].astype(BF16)
    down = lax.dot_general(hid[...], sel[:, half:], ROWS_DIM, preferred_element_type=F32)
    down_out[0] = down.astype(BF16)


def fused(x, g, ids, gates, block_expert, wg, wu, wd):
    n_e = lax.axis_size("expert")
    tok, width = x.shape
    blocks, half, ff = wg.shape
    pair, n_z = 2 * tok, n_e // 2
    tokens = n_e * pair
    slots = n_e * 2 * SLOT
    total_rows = blocks * slots
    vmem, sem = pltpu.VMEM, pltpu.SemaphoreType.DMA
    flops = 2 * total_rows * half * ff * 5 + 6 * total_rows * tokens * half
    out, sel, dgu, hid = pl.pallas_call(
        functools.partial(route_kernel, n_e, slots),
        out_shape=(
            jax.ShapeDtypeStruct((tok, width), BF16),
            jax.ShapeDtypeStruct((total_rows, 2 * half), BF16),
            jax.ShapeDtypeStruct((total_rows, 2 * ff), BF16),
            jax.ShapeDtypeStruct((total_rows, ff), BF16),
        ),
        in_specs=[pl.BlockSpec(memory_space=pltpu.SMEM)]
        + [pl.BlockSpec(memory_space=vmem)] * 4
        + [pl.BlockSpec(memory_space=pl.ANY)] * 3,
        out_specs=(
            pl.BlockSpec(memory_space=vmem),
            pl.BlockSpec(memory_space=pl.ANY),
            pl.BlockSpec(memory_space=vmem),
            pl.BlockSpec(memory_space=vmem),
        ),
        scratch_shapes=[
            vmem((blocks, half, ff), BF16),
            vmem((blocks, half, ff), BF16),
            vmem((blocks, ff, half), BF16),
            vmem((2, tok, 2 * half + LANES), BF16),
            vmem((tokens, 2 * half + LANES), BF16),
            vmem((total_rows, tokens), BF16),
            vmem((total_rows, 2 * half), BF16),
            vmem((blocks, slots, 3 * ff), F32),
            vmem((blocks, slots, 3 * ff), F32),
            vmem((total_rows, half), BF16),
            vmem((tokens, half), F32),
            vmem((tokens, half), BF16),
        ]
        + [vmem((n_z, pair, half), BF16)] * 5
        + [
            vmem((pair, half), F32),
            vmem((2, tok, half), BF16),
            vmem((tok, half), BF16),
            sem((3, blocks)),
            sem,
            sem((2,)),
            sem((n_e,)),
            sem((n_z,)),
            sem((n_z,)),
            sem((n_z,)),
            sem((blocks,)),
            sem((blocks,)),
        ]
        + [sem((n_z,))] * 6
        + [sem((2,))],
        compiler_params=pltpu.CompilerParams(
            collective_id=0, has_side_effects=True, vmem_limit_bytes=56 * 1024 * 1024
        ),
        cost_estimate=pl.CostEstimate(
            flops=flops, bytes_accessed=3 * wg.size * 2, transcendentals=total_rows * ff
        ),
        name="route",
    )(block_expert, x, g, ids, gates, wg, wu, wd)
    grads = weight_grads(sel, dgu, hid, blocks, half, ff, slots)
    return (out,) + grads


def weight_grads(sel, dgu, hid, blocks, half, ff, slots):
    return pl.pallas_call(
        grads_kernel,
        grid=(blocks,),
        out_shape=(
            jax.ShapeDtypeStruct((blocks, half, ff), BF16),
            jax.ShapeDtypeStruct((blocks, half, ff), BF16),
            jax.ShapeDtypeStruct((blocks, ff, half), BF16),
        ),
        in_specs=[
            pl.BlockSpec((slots, 2 * half), lambda j: (j, 0)),
            pl.BlockSpec((slots, 2 * ff), lambda j: (j, 0)),
            pl.BlockSpec((slots, ff), lambda j: (j, 0)),
        ],
        out_specs=(
            pl.BlockSpec((1, half, ff), lambda j: (j, 0, 0)),
            pl.BlockSpec((1, half, ff), lambda j: (j, 0, 0)),
            pl.BlockSpec((1, ff, half), lambda j: (j, 0, 0)),
        ),
        compiler_params=pltpu.CompilerParams(vmem_limit_bytes=48 * 1024 * 1024),
        cost_estimate=pl.CostEstimate(
            flops=6 * blocks * slots * half * ff, bytes_accessed=6 * blocks * half * ff, transcendentals=0
        ),
        name="weight_grads",
    )(sel, dgu, hid)


def spread(x, g, ids, gates, block_expert, wg, wu, wd):
    n_e, n_dp = lax.axis_size("expert"), lax.axis_size("dp")
    tok, width = x.shape
    blocks, half, ff = wg.shape
    slots = n_e * n_dp * SLOT
    tokens = n_e * n_dp * tok
    scaled = (gates.astype(F32) * g.astype(F32)).astype(BF16)
    both = lax.all_to_all(jnp.stack([x, scaled]), "dp", split_axis=2, concat_axis=1, tiled=True)
    both = lax.all_gather(both, "expert", axis=1, tiled=True)
    ids = lax.all_gather(ids.astype(BF16), ("expert", "dp"), axis=0, tiled=True)
    ids = ids.astype(jnp.int32)[:, 0]
    experts = lax.dynamic_slice_in_dim(block_expert, lax.axis_index("expert") * blocks, blocks)
    hits = experts[:, None] == ids[None, :]
    rank = jnp.cumsum(hits.astype(jnp.int32), axis=1) - 1
    place = jnp.arange(slots, dtype=jnp.int32)
    pick = hits[:, None, :] & (rank[:, None, :] == place[None, :, None])
    pick = pick.astype(BF16).reshape(blocks * slots, tokens)
    xs = jnp.dot(pick, both[0], preferred_element_type=F32).astype(BF16).reshape(blocks, slots, half)
    gs = jnp.dot(pick, both[1], preferred_element_type=F32).astype(BF16).reshape(blocks, slots, half)
    pre = jnp.stack([
        jnp.einsum("jrd,jdf->jrf", xs, wg, preferred_element_type=F32),
        jnp.einsum("jrd,jdf->jrf", xs, wu, preferred_element_type=F32),
        jnp.einsum("jrd,jfd->jrf", gs, wd, preferred_element_type=F32),
    ])
    pre = lax.psum(pre, "dp")
    hidden, d_gate, d_up = activations(pre[0], pre[1], pre[2])
    gate_grad = jnp.einsum("jrd,jrf->jdf", xs, d_gate, preferred_element_type=F32)
    up_grad = jnp.einsum("jrd,jrf->jdf", xs, d_up, preferred_element_type=F32)
    down_grad = jnp.einsum("jrf,jrd->jfd", hidden, gs, preferred_element_type=F32)
    part = jnp.einsum("jrf,jdf->jrd", d_gate, wg, preferred_element_type=F32)
    part = part + jnp.einsum("jrf,jdf->jrd", d_up, wu, preferred_element_type=F32)
    part = part.astype(BF16).reshape(blocks * slots, half)
    part = lax.dot_general(pick, part, ROWS_DIM, preferred_element_type=F32).astype(BF16)
    back = lax.all_to_all(part, ("expert", "dp"), split_axis=0, concat_axis=0, tiled=True)
    back = jnp.sum(back.reshape(n_e, n_dp, tok, half).astype(F32), axis=0)
    out = back.transpose(1, 0, 2).reshape(tok, width).astype(BF16)
    return out, gate_grad.astype(BF16), up_grad.astype(BF16), down_grad.astype(BF16)


def per_device(x, *rest):
    n_e, n_dp = lax.axis_size("expert"), lax.axis_size("dp")
    fits = n_dp == 2 and n_e % 2 == 0 and n_e * n_dp * x.shape[0] <= 512
    return fused(x, *rest) if fits else spread(x, *rest)


def solution(mesh):
    rows = P(("groups", "expert", "dp"), None)
    return jax.shard_map(
        per_device,
        mesh=mesh,
        in_specs=(
            rows,
            rows,
            rows,
            rows,
            P(),
            P("expert", "dp", None),
            P("expert", "dp", None),
            P("expert", None, "dp"),
        ),
        out_specs=(
            rows,
            P(("groups", "expert"), "dp", None),
            P(("groups", "expert"), "dp", None),
            P(("groups", "expert"), None, "dp"),
        ),
        check_vma=False,
    )
```

```python
import functools

import jax
import jax.numpy as jnp
from jax import lax
from jax.experimental import pallas as pl
from jax.experimental.pallas import tpu as pltpu
from jax.sharding import PartitionSpec as P

SLOT = 2
F32 = jnp.float32
BF16 = jnp.bfloat16
LANES = 128
ROWS_DIM = (((0,), (0,)), ((), ()))
LAST_DIM = (((1,), (1,)), ((), ()))


def activations(gate_pre, up_pre, hidden_grad):
    s = jax.nn.sigmoid(gate_pre)
    swish = gate_pre * s
    hidden = (swish * up_pre).astype(BF16)
    d_gate = (hidden_grad * up_pre * s * (1.0 + gate_pre * (1.0 - s))).astype(BF16)
    d_up = (hidden_grad * swish).astype(BF16)
    return hidden, d_gate, d_up


def tile_of(width):
    for tile in (256, 128):
        if width % tile == 0:
            return tile
    return width


def route_kernel(
    n_e, slots, parts,
    experts, x_ref, g_ref, ids_ref, gates_ref, wg_hbm, wu_hbm, wd_hbm,
    out_ref, sel_hbm, dgu_ref, hid_ref,
    wgu, wd, pack, buf, pick, sel, pre, pre_in, grad, grad_in, part_rows, total, sent,
    x_in, fin_out, fin_in,
    w_sem, sel_sem, pair_sem, recv_sem, x_sem, up_sem, down_sem, pre_sem, pre_recv,
    grad_sem, grad_recv, xs_sem, xs_recv, fin_sem, fin_recv,
):
    blocks, ff, half = wd.shape
    tok = x_ref.shape[0]
    pair = 2 * tok
    tokens = n_e * pair
    n_z = n_e // 2
    me, d = lax.axis_index("expert"), lax.axis_index("dp")
    z, col = me // 2, me % 2
    has_up, has_down = z < n_z - 1, z > 0
    core = {"dp": 1 - d}
    side = {"expert": me + 1 - 2 * col}
    above = {"expert": jnp.minimum(me + 2, n_e - 2 + col)}
    below = {"expert": jnp.maximum(me - 2, col)}

    def weight_copies(j):
        return [
            pltpu.make_async_copy(wg_hbm.at[j], wgu.at[j, :, 0:ff], w_sem.at[0, j]),
            pltpu.make_async_copy(wu_hbm.at[j], wgu.at[j, :, ff:2 * ff], w_sem.at[1, j]),
            pltpu.make_async_copy(wd_hbm.at[j], wd.at[j], w_sem.at[2, j]),
        ]

    def remote(src, dst, send, recv, where):
        return pltpu.make_async_remote_copy(
            src_ref=src, dst_ref=dst, send_sem=send, recv_sem=recv,
            device_id=where, device_id_type=pl.DeviceIdType.MESH,
        )

    barrier = pltpu.get_barrier_semaphore()
    for where in (core, side):
        pl.semaphore_signal(barrier, inc=1, device_id=where, device_id_type=pl.DeviceIdType.MESH)

    @pl.when(has_up)
    def _():
        pl.semaphore_signal(barrier, inc=1, device_id=above, device_id_type=pl.DeviceIdType.MESH)

    @pl.when(has_down)
    def _():
        pl.semaphore_signal(barrier, inc=1, device_id=below, device_id_type=pl.DeviceIdType.MESH)

    diagonal = lax.broadcasted_iota(jnp.int32, (tok, tok), 0) == lax.broadcasted_iota(
        jnp.int32, (tok, tok), 1
    )

    def column(ref):
        spread_row = jnp.broadcast_to(ref[...].astype(F32), (tok, tok))
        return jnp.sum(jnp.where(diagonal, spread_row, 0.0), axis=1, keepdims=True)

    g_at = half + LANES
    scaled = (column(gates_ref) * g_ref[...].astype(F32)).astype(BF16)
    named = jnp.broadcast_to(column(ids_ref), (tok, LANES)).astype(BF16)
    for h in range(2):
        pack[h, :, 0:half] = x_ref[:, h * half:(h + 1) * half]
        pack[h, :, half:g_at] = named
        pack[h, :, g_at:] = scaled[:, h * half:(h + 1) * half]

    pl.semaphore_wait(barrier, 2 + has_up.astype(jnp.int32) + has_down.astype(jnp.int32))

    mine = pl.ds(pl.multiple_of(me * pair + d * tok, 16), tok)
    swap = remote(pack.at[1 - d], buf.at[mine], pair_sem.at[0], pair_sem.at[1], core)
    swap.start()
    buf[mine, :] = pack[d]

    @pl.loop(0, blocks)
    def _(j):
        for copy in weight_copies(j):
            copy.start()

    swap.wait()

    def rows(b):
        return pl.ds(pl.multiple_of(b * pair, 16), pair)

    widths = ((0, g_at), (g_at, half))

    def hop(q, b, send, where):
        at = buf.at[rows(b), pl.ds(*widths[q])]
        return remote(at, at, send.at[q, b // 2], recv_sem.at[q, b], where)

    def gather_start(q):
        hop(q, me, x_sem, side).start()

        @pl.when(has_up)
        def _():
            hop(q, me, up_sem, above).start()

        @pl.when(has_down)
        def _():
            hop(q, me, down_sem, below).start()

    def gather_step(q, h):
        @pl.when(z - h >= 0)
        def _():
            b = me - 2 * h
            hop(q, b, x_sem, side).wait_recv()

            @pl.when(has_up)
            def _():
                hop(q, b, up_sem, above).start()

            hop(q, b, x_sem, side).start()

        @pl.when(z + h < n_z)
        def _():
            b = me + 2 * h
            hop(q, b, x_sem, side).wait_recv()

            @pl.when(has_down)
            def _():
                hop(q, b, down_sem, below).start()

            hop(q, b, x_sem, side).start()

    def gather_end(q):
        for k in range(n_z):
            hop(q, 2 * k + 1 - col, x_sem, side).wait_recv()

    gather_start(0)
    gather_start(1)
    for h in range(1, n_z):
        gather_step(0, h)
        if h == 2:
            gather_step(1, 1)
    gather_end(0)

    id_cols = buf[:, half:g_at].astype(F32)
    id_row = id_cols.T[0:1, :]
    earlier = lax.broadcasted_iota(jnp.int32, (tokens, tokens), 0) < lax.broadcasted_iota(
        jnp.int32, (tokens, tokens), 1
    )
    same = (id_cols[:, 0:1] == id_row) & earlier
    rank = jnp.sum(same.astype(F32), axis=0, keepdims=True)
    key = id_row * float(slots) + rank
    place = lax.broadcasted_iota(jnp.int32, (slots, tokens), 0).astype(F32)
    for j in range(blocks):
        base = experts[me * blocks + j].astype(F32) * float(slots)
        pick[j * slots:(j + 1) * slots, :] = (key == place + base).astype(F32).astype(BF16)

    step = tile_of(half)

    def select(source, target):
        @pl.loop(0, half // step)
        def _(c):
            src = pl.ds(pl.multiple_of(source + c * step, LANES), step)
            dst = pl.ds(pl.multiple_of(target + c * step, LANES), step)
            sel[:, dst] = jnp.dot(pick[...], buf[:, src], preferred_element_type=F32).astype(BF16)

    def slot_rows(j, count=1):
        return pl.ds(pl.multiple_of(j * slots, 16), count * slots)

    def swap_pre(j):
        return remote(pre.at[j], pre_in.at[j], pre_sem.at[j], pre_recv.at[j], core)

    def swap_grad(p):
        return remote(grad.at[p], grad_in.at[p], grad_sem.at[p], grad_recv.at[p], core)

    def forward(lo, hi):
        @pl.loop(lo, hi)
        def _(j):
            for copy in weight_copies(j)[:2]:
                copy.wait()
            pre[j] = jnp.dot(sel[slot_rows(j), 0:half], wgu[j], preferred_element_type=F32)
            swap_pre(j).start()

    late = [h for h in range(1, n_z) if not (h == 1 and n_z > 2)]
    select(0, 0)
    cuts = [blocks * i // max(1, len(late)) for i in range(len(late) + 1)]
    for i, h in enumerate(late):
        gather_step(1, h)
        forward(cuts[i], cuts[i + 1])
    if not late:
        forward(0, blocks)
    gather_end(1)
    select(g_at, half)

    sel_copy = pltpu.make_async_copy(sel, sel_hbm, sel_sem)
    sel_copy.start()

    @pl.loop(0, blocks // 2)
    def _(p):
        for b in range(2):
            weight_copies(2 * p + b)[2].wait()
        gs = sel[slot_rows(2 * p, 2), half:2 * half]
        down = wd[pl.ds(2 * p, 2)].reshape(2 * ff, half)
        both = lax.dot_general(gs, down, LAST_DIM, preferred_element_type=F32)
        grad[p, 0] = both[0:slots, 0:ff]
        grad[p, 1] = both[slots:, ff:]
        swap_grad(p).start()

    def block_rows(j, lo, hi):
        at = slot_rows(j)
        part = lax.dot_general(dgu_ref[at, :], wgu[j, lo:hi, :], LAST_DIM, preferred_element_type=F32)
        part_rows[at, lo:hi] = part.astype(BF16)

    def combine(lo, hi):
        for at in range(lo, hi, step):
            cols = slice(at, at + step)
            tile = lax.dot_general(pick[...], part_rows[:, cols], ROWS_DIM, preferred_element_type=F32)
            total[:, cols] = tile
            sent[:, cols] = tile.astype(BF16)

    def side_send(i, k):
        cols = pl.ds(parts[i], parts[i + 1] - parts[i])
        return remote(
            sent.at[rows(2 * k + 1 - col), cols], x_in.at[k, :, cols],
            xs_sem.at[i, k], xs_recv.at[i, k], side,
        )

    @pl.loop(0, blocks // 2)
    def _(p):
        swap_grad(p).wait()
        for b in range(2):
            j = 2 * p + b
            swap_pre(j).wait()
            both = pre[j] + pre_in[j]
            hidden_grad = grad[p, b] + grad_in[p, b]
            hidden, d_gate, d_up = activations(both[:, 0:ff], both[:, ff:], hidden_grad)
            at = slot_rows(j)
            hid_ref[at, :] = hidden
            dgu_ref[at, 0:ff] = d_gate
            dgu_ref[at, ff:] = d_up
            block_rows(j, parts[0], parts[1])

    for i in range(len(parts) - 1):
        if i > 0:
            @pl.loop(0, blocks // 2)
            def _(p):
                for b in range(2):
                    block_rows(2 * p + b, parts[i], parts[i + 1])

        combine(parts[i], parts[i + 1])
        for k in range(n_z):
            side_send(i, k).start()

    def swap_fin(k):
        return remote(fin_out.at[k, 1 - d], fin_in.at[k], fin_sem.at[k], fin_recv.at[k], core)

    for k in range(n_z):
        for i in range(len(parts) - 1):
            side_send(i, k).wait_recv()
        both = total[rows(2 * k + col), :] + x_in[k].astype(F32)
        fin_out[k] = both.astype(BF16).reshape(2, tok, half)
        swap_fin(k).start()
        out_ref[k, :, pl.ds(pl.multiple_of(d * half, LANES), half)] = fin_out[k, d]
    for k in range(n_z):
        swap_fin(k).wait()
        out_ref[k, :, pl.ds(pl.multiple_of((1 - d) * half, LANES), half)] = fin_in[k]

    for k in range(n_z):
        for i in range(len(parts) - 1):
            side_send(i, k).wait_send()
        for q in range(2):
            hop(q, 2 * k + col, x_sem, side).wait_send()

            @pl.when(has_up & (z >= k))
            def _():
                hop(q, 2 * k + col, up_sem, above).wait_send()

            @pl.when(has_down & (z <= k))
            def _():
                hop(q, 2 * k + col, down_sem, below).wait_send()

    sel_copy.wait()


def grads_kernel(sel, dgu, hid, gate_out, up_out, down_out):
    group, half, ff = gate_out.shape
    slots = sel.shape[0] // group
    for b in range(group):
        at = slice(b * slots, (b + 1) * slots)
        both = lax.dot_general(sel[at, 0:half], dgu[at, :], ROWS_DIM, preferred_element_type=F32)
        gate_out[b] = both[:, 0:ff].astype(BF16)
        up_out[b] = both[:, ff:].astype(BF16)
        down = lax.dot_general(hid[at, :], sel[at, half:], ROWS_DIM, preferred_element_type=F32)
        down_out[b] = down.astype(BF16)


def fused(x, g, ids, gates, block_expert, wg, wu, wd):
    n_e = lax.axis_size("expert")
    tok, width = x.shape
    blocks, half, ff = wg.shape
    pair, n_z = 2 * tok, n_e // 2
    tokens = n_e * pair
    slots = n_e * 2 * SLOT
    total_rows = blocks * slots
    vmem, sem = pltpu.VMEM, pltpu.SemaphoreType.DMA
    step = tile_of(half)
    middle = (half // step + 1) // 2 * step
    parts = (0, middle, half) if middle < half else (0, half)
    n_parts = len(parts) - 1
    flops = 2 * total_rows * half * ff * 5 + 6 * total_rows * tokens * half
    out, sel, dgu, hid = pl.pallas_call(
        functools.partial(route_kernel, n_e, slots, parts),
        out_shape=(
            jax.ShapeDtypeStruct((n_z, tok, width), BF16),
            jax.ShapeDtypeStruct((total_rows, 2 * half), BF16),
            jax.ShapeDtypeStruct((total_rows, 2 * ff), BF16),
            jax.ShapeDtypeStruct((total_rows, ff), BF16),
        ),
        in_specs=[pl.BlockSpec(memory_space=pltpu.SMEM)]
        + [pl.BlockSpec(memory_space=vmem)] * 4
        + [pl.BlockSpec(memory_space=pl.ANY)] * 3,
        out_specs=(
            pl.BlockSpec(memory_space=vmem),
            pl.BlockSpec(memory_space=pl.ANY),
            pl.BlockSpec(memory_space=vmem),
            pl.BlockSpec(memory_space=vmem),
        ),
        scratch_shapes=[
            vmem((blocks, half, 2 * ff), BF16),
            vmem((blocks, ff, half), BF16),
            vmem((2, tok, 2 * half + LANES), BF16),
            vmem((tokens, 2 * half + LANES), BF16),
            vmem((total_rows, tokens), BF16),
            vmem((total_rows, 2 * half), BF16),
            vmem((blocks, slots, 2 * ff), F32),
            vmem((blocks, slots, 2 * ff), F32),
            vmem((blocks // 2, 2, slots, ff), F32),
            vmem((blocks // 2, 2, slots, ff), F32),
            vmem((total_rows, half), BF16),
            vmem((tokens, half), F32),
            vmem((tokens, half), BF16),
            vmem((n_z, pair, half), BF16),
            vmem((n_z, 2, tok, half), BF16),
            vmem((n_z, tok, half), BF16),
            sem((3, blocks)),
            sem,
            sem((2,)),
            sem((2, n_e)),
            sem((2, n_z)),
            sem((2, n_z)),
            sem((2, n_z)),
            sem((blocks,)),
            sem((blocks,)),
            sem((blocks // 2,)),
            sem((blocks // 2,)),
            sem((n_parts, n_z)),
            sem((n_parts, n_z)),
            sem((n_z,)),
            sem((n_z,)),
        ],
        compiler_params=pltpu.CompilerParams(
            collective_id=0, has_side_effects=True, vmem_limit_bytes=56 * 1024 * 1024
        ),
        cost_estimate=pl.CostEstimate(
            flops=flops, bytes_accessed=3 * wg.size * 2, transcendentals=total_rows * ff
        ),
        name="route",
    )(block_expert, x, g, ids.reshape(1, tok), gates.reshape(1, tok), wg, wu, wd)
    lines = [list(range(col, n_e, 2)) for col in range(2)]
    out = lax.all_to_all(
        out, "expert", split_axis=0, concat_axis=0, tiled=True, axis_index_groups=lines
    )
    grads = weight_grads(sel, dgu, hid, blocks, half, ff, slots)
    return (jnp.sum(out.astype(F32), axis=0).astype(BF16),) + grads


def weight_grads(sel, dgu, hid, blocks, half, ff, slots):
    group = 4 if blocks % 4 == 0 else 1
    return pl.pallas_call(
        grads_kernel,
        grid=(blocks // group,),
        out_shape=(
            jax.ShapeDtypeStruct((blocks, half, ff), BF16),
            jax.ShapeDtypeStruct((blocks, half, ff), BF16),
            jax.ShapeDtypeStruct((blocks, ff, half), BF16),
        ),
        in_specs=[
            pl.BlockSpec((group * slots, 2 * half), lambda j: (j, 0)),
            pl.BlockSpec((group * slots, 2 * ff), lambda j: (j, 0)),
            pl.BlockSpec((group * slots, ff), lambda j: (j, 0)),
        ],
        out_specs=(
            pl.BlockSpec((group, half, ff), lambda j: (j, 0, 0)),
            pl.BlockSpec((group, half, ff), lambda j: (j, 0, 0)),
            pl.BlockSpec((group, ff, half), lambda j: (j, 0, 0)),
        ),
        compiler_params=pltpu.CompilerParams(vmem_limit_bytes=60 * 1024 * 1024),
        cost_estimate=pl.CostEstimate(
            flops=6 * blocks * slots * half * ff, bytes_accessed=6 * blocks * half * ff, transcendentals=0
        ),
        name="weight_grads",
    )(sel, dgu, hid)


def spread(x, g, ids, gates, block_expert, wg, wu, wd):
    n_e, n_dp = lax.axis_size("expert"), lax.axis_size("dp")
    tok, width = x.shape
    blocks, half, ff = wg.shape
    slots = n_e * n_dp * SLOT
    tokens = n_e * n_dp * tok
    scaled = (gates.astype(F32) * g.astype(F32)).astype(BF16)
    both = lax.all_to_all(jnp.stack([x, scaled]), "dp", split_axis=2, concat_axis=1, tiled=True)
    both = lax.all_gather(both, "expert", axis=1, tiled=True)
    ids = lax.all_gather(ids.astype(BF16), ("expert", "dp"), axis=0, tiled=True)
    ids = ids.astype(jnp.int32)[:, 0]
    experts = lax.dynamic_slice_in_dim(block_expert, lax.axis_index("expert") * blocks, blocks)
    hits = experts[:, None] == ids[None, :]
    rank = jnp.cumsum(hits.astype(jnp.int32), axis=1) - 1
    place = jnp.arange(slots, dtype=jnp.int32)
    pick = hits[:, None, :] & (rank[:, None, :] == place[None, :, None])
    pick = pick.astype(BF16).reshape(blocks * slots, tokens)
    xs = jnp.dot(pick, both[0], preferred_element_type=F32).astype(BF16).reshape(blocks, slots, half)
    gs = jnp.dot(pick, both[1], preferred_element_type=F32).astype(BF16).reshape(blocks, slots, half)
    pre = jnp.stack([
        jnp.einsum("jrd,jdf->jrf", xs, wg, preferred_element_type=F32),
        jnp.einsum("jrd,jdf->jrf", xs, wu, preferred_element_type=F32),
        jnp.einsum("jrd,jfd->jrf", gs, wd, preferred_element_type=F32),
    ])
    pre = lax.psum(pre, "dp")
    hidden, d_gate, d_up = activations(pre[0], pre[1], pre[2])
    gate_grad = jnp.einsum("jrd,jrf->jdf", xs, d_gate, preferred_element_type=F32)
    up_grad = jnp.einsum("jrd,jrf->jdf", xs, d_up, preferred_element_type=F32)
    down_grad = jnp.einsum("jrf,jrd->jfd", hidden, gs, preferred_element_type=F32)
    part = jnp.einsum("jrf,jdf->jrd", d_gate, wg, preferred_element_type=F32)
    part = part + jnp.einsum("jrf,jdf->jrd", d_up, wu, preferred_element_type=F32)
    part = part.astype(BF16).reshape(blocks * slots, half)
    part = lax.dot_general(pick, part, ROWS_DIM, preferred_element_type=F32).astype(BF16)
    back = lax.all_to_all(part, ("expert", "dp"), split_axis=0, concat_axis=0, tiled=True)
    back = jnp.sum(back.reshape(n_e, n_dp, tok, half).astype(F32), axis=0)
    out = back.transpose(1, 0, 2).reshape(tok, width).astype(BF16)
    return out, gate_grad.astype(BF16), up_grad.astype(BF16), down_grad.astype(BF16)


def per_device(x, *rest):
    n_e, n_dp = lax.axis_size("expert"), lax.axis_size("dp")
    fits = n_dp == 2 and n_e % 2 == 0 and rest[4].shape[0] % 2 == 0 and n_e * n_dp * x.shape[0] <= 512
    return fused(x, *rest) if fits else spread(x, *rest)


def solution(mesh):
    rows = P(("groups", "expert", "dp"), None)
    return jax.shard_map(
        per_device,
        mesh=mesh,
        in_specs=(
            rows,
            rows,
            rows,
            rows,
            P(),
            P("expert", "dp", None),
            P("expert", "dp", None),
            P("expert", None, "dp"),
        ),
        out_specs=(
            rows,
            P(("groups", "expert"), "dp", None),
            P(("groups", "expert"), "dp", None),
            P(("groups", "expert"), None, "dp"),
        ),
        check_vma=False,
    )
```

```python
import jax
import jax.numpy as jnp
from jax import lax
from jax.experimental import pallas as pl
from jax.experimental.pallas import tpu as pltpu
from jax.sharding import PartitionSpec as P

SLOT = 2
F32 = jnp.float32
BF16 = jnp.bfloat16
LANES = 128
ROWS_DIM = (((0,), (0,)), ((), ()))
LAST_DIM = (((1,), (1,)), ((), ()))


def activations(gate_pre, up_pre, hidden_grad):
    s = jax.nn.sigmoid(gate_pre)
    swish = gate_pre * s
    hidden = (swish * up_pre).astype(BF16)
    d_gate = (hidden_grad * up_pre * s * (1.0 + gate_pre * (1.0 - s))).astype(BF16)
    d_up = (hidden_grad * swish).astype(BF16)
    return hidden, d_gate, d_up


def tile_of(width):
    for tile in (256, 128):
        if width % tile == 0:
            return tile
    return width


def route_kernel(
    n_e, slots, parts,
    experts, x_ref, g_ref, ids_ref, gates_ref, wg_hbm, wu_hbm, wd_hbm,
    outs, sel_hbm, dgu_ref, hid_ref,
    wgu, wd, pack, buf, pick, sel, pre, pre_in, grad, grad_in, part_rows, total, sent,
    x_in, fin_out, fin_in,
    w_sem, sel_sem, pair_sem, recv_sem, x_sem, up_sem, down_sem, pre_sem, pre_recv,
    grad_sem, grad_recv, xs_sem, xs_recv, fin_sem, fin_recv,
):
    blocks, ff, half = wd.shape
    tok = x_ref.shape[0]
    pair = 2 * tok
    tokens = n_e * pair
    n_z = n_e // 2
    me, d = lax.axis_index("expert"), lax.axis_index("dp")
    z, col = me // 2, me % 2
    has_up, has_down = z < n_z - 1, z > 0
    core = {"dp": 1 - d}
    side = {"expert": me + 1 - 2 * col}
    above = {"expert": jnp.minimum(me + 2, n_e - 2 + col)}
    below = {"expert": jnp.maximum(me - 2, col)}

    def weight_copies(j):
        return [
            pltpu.make_async_copy(wg_hbm.at[j], wgu.at[j, :, 0:ff], w_sem.at[0, j]),
            pltpu.make_async_copy(wu_hbm.at[j], wgu.at[j, :, ff:2 * ff], w_sem.at[1, j]),
            pltpu.make_async_copy(wd_hbm.at[j], wd.at[j], w_sem.at[2, j]),
        ]

    def remote(src, dst, send, recv, where):
        return pltpu.make_async_remote_copy(
            src_ref=src, dst_ref=dst, send_sem=send, recv_sem=recv,
            device_id=where, device_id_type=pl.DeviceIdType.MESH,
        )

    barrier = pltpu.get_barrier_semaphore()
    for where in (core, side):
        pl.semaphore_signal(barrier, inc=1, device_id=where, device_id_type=pl.DeviceIdType.MESH)

    @pl.when(has_up)
    def _():
        pl.semaphore_signal(barrier, inc=1, device_id=above, device_id_type=pl.DeviceIdType.MESH)

    @pl.when(has_down)
    def _():
        pl.semaphore_signal(barrier, inc=1, device_id=below, device_id_type=pl.DeviceIdType.MESH)

    diagonal = lax.broadcasted_iota(jnp.int32, (tok, tok), 0) == lax.broadcasted_iota(
        jnp.int32, (tok, tok), 1
    )

    def column(ref):
        spread_row = jnp.broadcast_to(ref[...].astype(F32), (tok, tok))
        return jnp.sum(jnp.where(diagonal, spread_row, 0.0), axis=1, keepdims=True)

    g_at = half + LANES
    scaled = (column(gates_ref) * g_ref[...].astype(F32)).astype(BF16)
    named = jnp.broadcast_to(column(ids_ref), (tok, LANES)).astype(BF16)
    for h in range(2):
        pack[h, :, 0:half] = x_ref[:, h * half:(h + 1) * half]
        pack[h, :, half:g_at] = named
        pack[h, :, g_at:] = scaled[:, h * half:(h + 1) * half]

    pl.semaphore_wait(barrier, 2 + has_up.astype(jnp.int32) + has_down.astype(jnp.int32))

    mine = pl.ds(pl.multiple_of(me * pair + d * tok, 16), tok)
    swap = remote(pack.at[1 - d], buf.at[mine], pair_sem.at[0], pair_sem.at[1], core)
    swap.start()
    buf[mine, :] = pack[d]

    @pl.loop(0, blocks)
    def _(j):
        for copy in weight_copies(j):
            copy.start()

    swap.wait()

    def rows(b):
        return pl.ds(pl.multiple_of(b * pair, 16), pair)

    widths = ((0, g_at), (g_at, half))

    def hop(q, b, send, where):
        at = buf.at[rows(b), pl.ds(*widths[q])]
        return remote(at, at, send.at[q, b // 2], recv_sem.at[q, b], where)

    def gather_start(q):
        hop(q, me, x_sem, side).start()

        @pl.when(has_up)
        def _():
            hop(q, me, up_sem, above).start()

        @pl.when(has_down)
        def _():
            hop(q, me, down_sem, below).start()

    def gather_step(q, h):
        @pl.when(z - h >= 0)
        def _():
            b = me - 2 * h
            hop(q, b, x_sem, side).wait_recv()

            @pl.when(has_up)
            def _():
                hop(q, b, up_sem, above).start()

            hop(q, b, x_sem, side).start()

        @pl.when(z + h < n_z)
        def _():
            b = me + 2 * h
            hop(q, b, x_sem, side).wait_recv()

            @pl.when(has_down)
            def _():
                hop(q, b, down_sem, below).start()

            hop(q, b, x_sem, side).start()

    def gather_end(q):
        for k in range(n_z):
            hop(q, 2 * k + 1 - col, x_sem, side).wait_recv()

    gather_start(0)
    gather_start(1)
    for h in range(1, n_z):
        gather_step(0, h)
        if h == 2:
            gather_step(1, 1)
    gather_end(0)

    id_cols = buf[:, half:g_at].astype(F32)
    id_row = id_cols.T[0:1, :]
    earlier = lax.broadcasted_iota(jnp.int32, (tokens, tokens), 0) < lax.broadcasted_iota(
        jnp.int32, (tokens, tokens), 1
    )
    same = (id_cols[:, 0:1] == id_row) & earlier
    rank = jnp.sum(same.astype(F32), axis=0, keepdims=True)
    key = id_row * float(slots) + rank
    place = lax.broadcasted_iota(jnp.int32, (slots, tokens), 0).astype(F32)
    for j in range(blocks):
        base = experts[me * blocks + j].astype(F32) * float(slots)
        pick[j * slots:(j + 1) * slots, :] = (key == place + base).astype(F32).astype(BF16)

    step = tile_of(half)

    def select(source, target):
        @pl.loop(0, half // step)
        def _(c):
            src = pl.ds(pl.multiple_of(source + c * step, LANES), step)
            dst = pl.ds(pl.multiple_of(target + c * step, LANES), step)
            sel[:, dst] = jnp.dot(pick[...], buf[:, src], preferred_element_type=F32).astype(BF16)

    def slot_rows(j, count=1):
        return pl.ds(pl.multiple_of(j * slots, 16), count * slots)

    def swap_pre(j):
        return remote(pre.at[j], pre_in.at[j], pre_sem.at[j], pre_recv.at[j], core)

    def swap_grad(p):
        return remote(grad.at[p], grad_in.at[p], grad_sem.at[p], grad_recv.at[p], core)

    def forward(lo, hi):
        @pl.loop(lo, hi)
        def _(j):
            for copy in weight_copies(j)[:2]:
                copy.wait()
            pre[j] = jnp.dot(sel[slot_rows(j), 0:half], wgu[j], preferred_element_type=F32)
            swap_pre(j).start()

    late = [h for h in range(1, n_z) if not (h == 1 and n_z > 2)]
    select(0, 0)
    cuts = [blocks * i // max(1, len(late)) for i in range(len(late) + 1)]
    for i, h in enumerate(late):
        gather_step(1, h)
        forward(cuts[i], cuts[i + 1])
    if not late:
        forward(0, blocks)
    gather_end(1)
    select(g_at, half)

    sel_copy = pltpu.make_async_copy(sel, sel_hbm, sel_sem)
    sel_copy.start()

    @pl.loop(0, blocks // 2)
    def _(p):
        for b in range(2):
            weight_copies(2 * p + b)[2].wait()
        gs = sel[slot_rows(2 * p, 2), half:2 * half]
        down = wd[pl.ds(2 * p, 2)].reshape(2 * ff, half)
        both = lax.dot_general(gs, down, LAST_DIM, preferred_element_type=F32)
        grad[p, 0] = both[0:slots, 0:ff]
        grad[p, 1] = both[slots:, ff:]
        swap_grad(p).start()

    def block_rows(j, lo, hi):
        at = slot_rows(j)
        part = lax.dot_general(dgu_ref[at, :], wgu[j, lo:hi, :], LAST_DIM, preferred_element_type=F32)
        part_rows[at, lo:hi] = part.astype(BF16)

    def combine(lo, hi):
        for at in range(lo, hi, step):
            cols = slice(at, at + step)
            tile = lax.dot_general(pick[...], part_rows[:, cols], ROWS_DIM, preferred_element_type=F32)
            total[:, cols] = tile
            sent[:, cols] = tile.astype(BF16)

    def side_send(i, k):
        cols = pl.ds(parts[i], parts[i + 1] - parts[i])
        return remote(
            sent.at[rows(2 * k + 1 - col), cols], x_in.at[k, :, cols],
            xs_sem.at[i, k], xs_recv.at[i, k], side,
        )

    @pl.loop(0, blocks // 2)
    def _(p):
        swap_grad(p).wait()
        for b in range(2):
            j = 2 * p + b
            swap_pre(j).wait()
            both = pre[j] + pre_in[j]
            hidden_grad = grad[p, b] + grad_in[p, b]
            hidden, d_gate, d_up = activations(both[:, 0:ff], both[:, ff:], hidden_grad)
            at = slot_rows(j)
            hid_ref[at, :] = hidden
            dgu_ref[at, 0:ff] = d_gate
            dgu_ref[at, ff:] = d_up
            block_rows(j, parts[0], parts[1])

    for i in range(len(parts) - 1):
        if i > 0:
            @pl.loop(0, blocks // 2)
            def _(p):
                for b in range(2):
                    block_rows(2 * p + b, parts[i], parts[i + 1])

        combine(parts[i], parts[i + 1])
        for k in range(n_z):
            side_send(i, k).start()

    def swap_fin(k):
        return remote(fin_out.at[k, 1 - d], fin_in.at[k], fin_sem.at[k], fin_recv.at[k], core)

    for o in range(n_z):
        k = lax.rem(z + o, n_z)
        for i in range(len(parts) - 1):
            side_send(i, k).wait_recv()
        both = total[rows(2 * k + col), :] + x_in[k].astype(F32)
        fin_out[k] = both.astype(BF16).reshape(2, tok, half)
        swap_fin(k).start()
        outs[o][:, pl.ds(pl.multiple_of(d * half, LANES), half)] = fin_out[k, d]
    for o in range(n_z):
        k = lax.rem(z + o, n_z)
        swap_fin(k).wait()
        outs[o][:, pl.ds(pl.multiple_of((1 - d) * half, LANES), half)] = fin_in[k]

    for k in range(n_z):
        for i in range(len(parts) - 1):
            side_send(i, k).wait_send()
        for q in range(2):
            hop(q, 2 * k + col, x_sem, side).wait_send()

            @pl.when(has_up & (z >= k))
            def _():
                hop(q, 2 * k + col, up_sem, above).wait_send()

            @pl.when(has_down & (z <= k))
            def _():
                hop(q, 2 * k + col, down_sem, below).wait_send()

    sel_copy.wait()


def grads_kernel(sel, dgu, hid, gate_out, up_out, down_out):
    group, half, ff = gate_out.shape
    slots = sel.shape[0] // group
    for b in range(group):
        at = slice(b * slots, (b + 1) * slots)
        both = lax.dot_general(sel[at, 0:half], dgu[at, :], ROWS_DIM, preferred_element_type=F32)
        gate_out[b] = both[:, 0:ff].astype(BF16)
        up_out[b] = both[:, ff:].astype(BF16)
        down = lax.dot_general(hid[at, :], sel[at, half:], ROWS_DIM, preferred_element_type=F32)
        down_out[b] = down.astype(BF16)


def fused(x, g, ids, gates, block_expert, wg, wu, wd):
    n_e = lax.axis_size("expert")
    tok, width = x.shape
    blocks, half, ff = wg.shape
    pair, n_z = 2 * tok, n_e // 2
    tokens = n_e * pair
    slots = n_e * 2 * SLOT
    total_rows = blocks * slots
    vmem, sem = pltpu.VMEM, pltpu.SemaphoreType.DMA
    step = tile_of(half)
    middle = (half // step + 1) // 2 * step
    parts = (0, middle, half) if middle < half else (0, half)
    n_parts = len(parts) - 1
    flops = 2 * total_rows * half * ff * 5 + 6 * total_rows * tokens * half

    def kernel(*refs):
        end = 8 + n_z
        route_kernel(n_e, slots, parts, *refs[:8], refs[8:end], *refs[end:])

    *sums, sel, dgu, hid = pl.pallas_call(
        kernel,
        out_shape=(
            *[jax.ShapeDtypeStruct((tok, width), BF16)] * n_z,
            jax.ShapeDtypeStruct((total_rows, 2 * half), BF16),
            jax.ShapeDtypeStruct((total_rows, 2 * ff), BF16),
            jax.ShapeDtypeStruct((total_rows, ff), BF16),
        ),
        in_specs=[pl.BlockSpec(memory_space=pltpu.SMEM)]
        + [pl.BlockSpec(memory_space=vmem)] * 4
        + [pl.BlockSpec(memory_space=pl.ANY)] * 3,
        out_specs=(
            *[pl.BlockSpec(memory_space=vmem)] * n_z,
            pl.BlockSpec(memory_space=pl.ANY),
            pl.BlockSpec(memory_space=vmem),
            pl.BlockSpec(memory_space=vmem),
        ),
        scratch_shapes=[
            vmem((blocks, half, 2 * ff), BF16),
            vmem((blocks, ff, half), BF16),
            vmem((2, tok, 2 * half + LANES), BF16),
            vmem((tokens, 2 * half + LANES), BF16),
            vmem((total_rows, tokens), BF16),
            vmem((total_rows, 2 * half), BF16),
            vmem((blocks, slots, 2 * ff), F32),
            vmem((blocks, slots, 2 * ff), F32),
            vmem((blocks // 2, 2, slots, ff), F32),
            vmem((blocks // 2, 2, slots, ff), F32),
            vmem((total_rows, half), BF16),
            vmem((tokens, half), F32),
            vmem((tokens, half), BF16),
            vmem((n_z, pair, half), BF16),
            vmem((n_z, 2, tok, half), BF16),
            vmem((n_z, tok, half), BF16),
            sem((3, blocks)),
            sem,
            sem((2,)),
            sem((2, n_e)),
            sem((2, n_z)),
            sem((2, n_z)),
            sem((2, n_z)),
            sem((blocks,)),
            sem((blocks,)),
            sem((blocks // 2,)),
            sem((blocks // 2,)),
            sem((n_parts, n_z)),
            sem((n_parts, n_z)),
            sem((n_z,)),
            sem((n_z,)),
        ],
        compiler_params=pltpu.CompilerParams(
            collective_id=0, has_side_effects=True, vmem_limit_bytes=56 * 1024 * 1024
        ),
        cost_estimate=pl.CostEstimate(
            flops=flops, bytes_accessed=3 * wg.size * 2, transcendentals=total_rows * ff
        ),
        name="route",
    )(block_expert, x, g, ids.reshape(1, tok), gates.reshape(1, tok), wg, wu, wd)
    for o in range(1, n_z):
        ring = [(e, (e + 2 * o) % n_e) for e in range(n_e)]
        sums[o] = lax.ppermute(sums[o], "expert", ring)
    grads = weight_grads(sel, dgu, hid, blocks, half, ff, slots)
    return (sum(part.astype(F32) for part in sums).astype(BF16),) + grads


def weight_grads(sel, dgu, hid, blocks, half, ff, slots):
    group = 4 if blocks % 4 == 0 else 1
    return pl.pallas_call(
        grads_kernel,
        grid=(blocks // group,),
        out_shape=(
            jax.ShapeDtypeStruct((blocks, half, ff), BF16),
            jax.ShapeDtypeStruct((blocks, half, ff), BF16),
            jax.ShapeDtypeStruct((blocks, ff, half), BF16),
        ),
        in_specs=[
            pl.BlockSpec((group * slots, 2 * half), lambda j: (j, 0)),
            pl.BlockSpec((group * slots, 2 * ff), lambda j: (j, 0)),
            pl.BlockSpec((group * slots, ff), lambda j: (j, 0)),
        ],
        out_specs=(
            pl.BlockSpec((group, half, ff), lambda j: (j, 0, 0)),
            pl.BlockSpec((group, half, ff), lambda j: (j, 0, 0)),
            pl.BlockSpec((group, ff, half), lambda j: (j, 0, 0)),
        ),
        compiler_params=pltpu.CompilerParams(vmem_limit_bytes=60 * 1024 * 1024),
        cost_estimate=pl.CostEstimate(
            flops=6 * blocks * slots * half * ff, bytes_accessed=6 * blocks * half * ff, transcendentals=0
        ),
        name="weight_grads",
    )(sel, dgu, hid)


def spread(x, g, ids, gates, block_expert, wg, wu, wd):
    n_e, n_dp = lax.axis_size("expert"), lax.axis_size("dp")
    tok, width = x.shape
    blocks, half, ff = wg.shape
    slots = n_e * n_dp * SLOT
    tokens = n_e * n_dp * tok
    scaled = (gates.astype(F32) * g.astype(F32)).astype(BF16)
    both = lax.all_to_all(jnp.stack([x, scaled]), "dp", split_axis=2, concat_axis=1, tiled=True)
    both = lax.all_gather(both, "expert", axis=1, tiled=True)
    ids = lax.all_gather(ids.astype(BF16), ("expert", "dp"), axis=0, tiled=True)
    ids = ids.astype(jnp.int32)[:, 0]
    experts = lax.dynamic_slice_in_dim(block_expert, lax.axis_index("expert") * blocks, blocks)
    hits = experts[:, None] == ids[None, :]
    rank = jnp.cumsum(hits.astype(jnp.int32), axis=1) - 1
    place = jnp.arange(slots, dtype=jnp.int32)
    pick = hits[:, None, :] & (rank[:, None, :] == place[None, :, None])
    pick = pick.astype(BF16).reshape(blocks * slots, tokens)
    xs = jnp.dot(pick, both[0], preferred_element_type=F32).astype(BF16).reshape(blocks, slots, half)
    gs = jnp.dot(pick, both[1], preferred_element_type=F32).astype(BF16).reshape(blocks, slots, half)
    pre = jnp.stack([
        jnp.einsum("jrd,jdf->jrf", xs, wg, preferred_element_type=F32),
        jnp.einsum("jrd,jdf->jrf", xs, wu, preferred_element_type=F32),
        jnp.einsum("jrd,jfd->jrf", gs, wd, preferred_element_type=F32),
    ])
    pre = lax.psum(pre, "dp")
    hidden, d_gate, d_up = activations(pre[0], pre[1], pre[2])
    gate_grad = jnp.einsum("jrd,jrf->jdf", xs, d_gate, preferred_element_type=F32)
    up_grad = jnp.einsum("jrd,jrf->jdf", xs, d_up, preferred_element_type=F32)
    down_grad = jnp.einsum("jrf,jrd->jfd", hidden, gs, preferred_element_type=F32)
    part = jnp.einsum("jrf,jdf->jrd", d_gate, wg, preferred_element_type=F32)
    part = part + jnp.einsum("jrf,jdf->jrd", d_up, wu, preferred_element_type=F32)
    part = part.astype(BF16).reshape(blocks * slots, half)
    part = lax.dot_general(pick, part, ROWS_DIM, preferred_element_type=F32).astype(BF16)
    back = lax.all_to_all(part, ("expert", "dp"), split_axis=0, concat_axis=0, tiled=True)
    back = jnp.sum(back.reshape(n_e, n_dp, tok, half).astype(F32), axis=0)
    out = back.transpose(1, 0, 2).reshape(tok, width).astype(BF16)
    return out, gate_grad.astype(BF16), up_grad.astype(BF16), down_grad.astype(BF16)


def per_device(x, *rest):
    n_e, n_dp = lax.axis_size("expert"), lax.axis_size("dp")
    fits = n_dp == 2 and n_e % 2 == 0 and rest[4].shape[0] % 2 == 0 and n_e * n_dp * x.shape[0] <= 512
    return fused(x, *rest) if fits else spread(x, *rest)


def solution(mesh):
    rows = P(("groups", "expert", "dp"), None)
    return jax.shard_map(
        per_device,
        mesh=mesh,
        in_specs=(
            rows,
            rows,
            rows,
            rows,
            P(),
            P("expert", "dp", None),
            P("expert", "dp", None),
            P("expert", None, "dp"),
        ),
        out_specs=(
            rows,
            P(("groups", "expert"), "dp", None),
            P(("groups", "expert"), "dp", None),
            P(("groups", "expert"), None, "dp"),
        ),
        check_vma=False,
    )
```
